32 devices in a mesh: groups: 2 (over x), dp: 16 (over z, y, core).
Axes of the slice: x: 2, y: 2, z: 4, core: 2. Of those that a mesh axis runs over, the one named last changes fastest.
Arguments:
- activations: bfloat16 [128, 176, 4096], P(('groups', 'dp')), parts along dimension 0, may hold values from -6 to 6
- cotangent: bfloat16 [128, 176, 1024], P(('groups', 'dp')), parts along dimension 0, may hold values from -6 to 6
- lengths: int32 [128], P(('groups', 'dp')), parts along dimension 0, may hold values from 44 to 176, as said below
- handover: int32 [128], P(('groups', 'dp')), parts along dimension 0, may hold values from 0 to 1, as said below
- adapter_down_factor: bfloat16 [64, 4096], replicated, may hold values from -0.09375 to 0.09375
- adapter_up_factor: bfloat16 [1024, 64], replicated, may hold values from -0.75 to 0.75
- output_feature_projection: bfloat16 [1024, 64], replicated, as said below
- up_rank_projection: bfloat16 [64, 64], replicated, as said below
- input_feature_projection: bfloat16 [4096, 64], replicated, as said below
- down_rank_projection: bfloat16 [64, 64], replicated, as said below
Outputs:
- feature_store: float32 [192, 8192], P(('groups', 'dp')), parts along dimension 0
- gram_panel: float32 [16384, 8192], P(('groups', 'dp')), parts along dimension 0
The draws below stay inside these ranges and needn't reach their ends.
There are 2 independent parts, one for each index of `groups`. The reference program is written for one: setup_inputs(seed, part) draws one part's arguments, and reference() takes and returns one part's arrays. A program takes and returns all parts, laid end to end along the dimension named above; an argument that names none is the same for every part. Nothing has to cross between parts.
Inputs may be any that keep to these rules, and one draw needn't show every extreme that they name: `lengths`: some example has exactly 176 live tokens. At most 2 of the 4 examples of one index of dp have handover 1, and some index has exactly 2. `output_feature_projection`: every entry is plus or minus one over the square root of the number of rows. `up_rank_projection`: every entry is plus or minus one over the square root of the number of rows. `input_feature_projection`: every entry is plus or minus one over the square root of the number of rows. `down_rank_projection`: every entry is plus or minus one over the square root of the number of rows.
All inputs are finite; a program needn't handle non-finite values.
Results may differ from the reference program's by a relative error of at most 0.007.
Values may be sent and summed in bfloat16 or wider, within the bound.
A program may use at most 128 MiB of HBM per device.

```python
import math
import jax
import jax.numpy as jnp
from jax import lax

MODEL_WIDTH = 4096
VALUE_OUT_WIDTH = 1024
ADAPTER_RANK = 64
PO = 64
E_DEV = 4
LCAP = 176
MOVED = 2
FEATURES = 8192
EXAMPLES = 64
STORE = 96
N_DP = 16


def signed_table(key, rows, columns):
    signs = jax.random.rademacher(key, (rows, columns), dtype=jnp.float32)
    return signs * rows ** (-0.5)


def draw_lengths(key, part):
    key = jax.random.fold_in(key, 11)
    key_one, key_two = jax.random.split(key)
    lowest = max(1, LCAP // 4)
    values = jax.random.randint(key_one, (EXAMPLES,), lowest, LCAP + 1, dtype=jnp.int32)
    chosen = jax.random.randint(key_two, (), 0, EXAMPLES, dtype=jnp.int32)
    return jnp.where(jnp.arange(EXAMPLES, dtype=jnp.int32) == chosen, LCAP, values).astype(jnp.int32)


def draw_handover(key, part):
    key = jax.random.fold_in(key, 23)
    key_one, key_two, key_three = jax.random.split(key, 3)
    counts = jax.random.randint(key_one, (N_DP,), 0, MOVED + 1, dtype=jnp.int32)
    full_device = jax.random.randint(key_two, (), 0, N_DP, dtype=jnp.int32)
    counts = jnp.where(jnp.arange(N_DP, dtype=jnp.int32) == full_device, MOVED, counts)
    scores = jax.random.randint(key_three, (N_DP, E_DEV), 0, 1 << 20, dtype=jnp.int32)
    scores = scores * E_DEV + jnp.arange(E_DEV, dtype=jnp.int32)[None, :]
    ranks = jnp.argsort(jnp.argsort(scores, axis=1, stable=True), axis=1, stable=True)
    return (ranks < counts[:, None]).astype(jnp.int32).reshape(EXAMPLES)


def draw_output_feature_projection(key, part):
    key = jax.random.fold_in(key, 31)
    return signed_table(key, VALUE_OUT_WIDTH, PO).astype(jnp.bfloat16)


def draw_up_rank_projection(key, part):
    key = jax.random.fold_in(key, 37)
    return signed_table(key, ADAPTER_RANK, PO).astype(jnp.bfloat16)


def draw_input_feature_projection(key, part):
    key = jax.random.fold_in(key, 41)
    return signed_table(key, MODEL_WIDTH, PO).astype(jnp.bfloat16)


def draw_down_rank_projection(key, part):
    key = jax.random.fold_in(key, 43)
    return signed_table(key, ADAPTER_RANK, PO).astype(jnp.bfloat16)


def level_of(key, extent, shards, low, largest):
    def one(axis_at, parts):
        steps = jax.random.uniform(jax.random.fold_in(jax.random.fold_in(key, 6), axis_at), (parts,), jnp.float32, low / len(shards), largest / len(shards))
        return jnp.repeat(jnp.exp(steps), extent[axis_at] // parts).reshape((-1,) + (1,) * (len(extent) - axis_at - 1))

    factor_of = one(*shards[0])
    for cut in shards[1:]:
        factor_of = factor_of * one(*cut)
    return factor_of


def gaussian(own_key, shape, scale, limit, pieces=(), kind=jnp.bfloat16):
    factor_of = level_of(own_key, shape, pieces, -0.22, 0.18) if pieces else 1.0
    array = jax.random.normal(own_key, shape, jnp.float32) * scale * factor_of
    return jnp.minimum(jnp.maximum(array, -limit), limit).astype(kind)


def setup_inputs(seed: int = 0, part: int = 0) -> dict:
    streams_of = jax.random.split(jax.random.key(seed), 11)
    own_keys = jax.random.split(jax.random.fold_in(streams_of[10], part), 11)
    activations = gaussian(own_keys[0], (EXAMPLES, LCAP, MODEL_WIDTH), 1.0, 6.0, ((0, 16),))
    cotangent = gaussian(own_keys[1], (EXAMPLES, LCAP, VALUE_OUT_WIDTH), 1.0, 6.0, ((0, 16),))
    lengths = draw_lengths(jax.random.fold_in(jax.random.fold_in(streams_of[10], part), 71), part)
    handover = draw_handover(jax.random.fold_in(jax.random.fold_in(streams_of[10], part), 71), part)
    adapter_down_factor = gaussian(streams_of[4], (ADAPTER_RANK, MODEL_WIDTH), MODEL_WIDTH ** -0.5, 0.09375)
    adapter_up_factor = gaussian(streams_of[5], (VALUE_OUT_WIDTH, ADAPTER_RANK), ADAPTER_RANK ** -0.5, 0.75)
    output_feature_projection = draw_output_feature_projection(jax.random.fold_in(streams_of[10], 71), part)
    up_rank_projection = draw_up_rank_projection(jax.random.fold_in(streams_of[10], 71), part)
    input_feature_projection = draw_input_feature_projection(jax.random.fold_in(streams_of[10], 71), part)
    down_rank_projection = draw_down_rank_projection(jax.random.fold_in(streams_of[10], 71), part)
    return dict(activations=activations, cotangent=cotangent, lengths=lengths, handover=handover, adapter_down_factor=adapter_down_factor, adapter_up_factor=adapter_up_factor, output_feature_projection=output_feature_projection, up_rank_projection=up_rank_projection, input_feature_projection=input_feature_projection, down_rank_projection=down_rank_projection)


def per_token_features(activations, cotangent, lengths, adapter_down_factor, adapter_up_factor, output_feature_projection, up_rank_projection, input_feature_projection, down_rank_projection):
    examples, span, width = activations.shape
    flat_activation_rows = activations.reshape(examples * span, width)
    flat_cotangent_rows = cotangent.reshape(examples * span, cotangent.shape[2])
    reduced_down_gradient = jnp.dot(flat_activation_rows, adapter_down_factor.T, preferred_element_type=jnp.float32).astype(jnp.bfloat16)
    in_side = jnp.dot(flat_activation_rows, input_feature_projection, preferred_element_type=jnp.float32).astype(jnp.bfloat16)
    reduced_up_gradient = jnp.dot(flat_cotangent_rows, adapter_up_factor, preferred_element_type=jnp.float32).astype(jnp.bfloat16)
    out_side = jnp.dot(flat_cotangent_rows, output_feature_projection, preferred_element_type=jnp.float32).astype(jnp.bfloat16)
    rank_b = jnp.dot(reduced_down_gradient, up_rank_projection, preferred_element_type=jnp.float32).astype(jnp.bfloat16)
    rank_a = jnp.dot(reduced_up_gradient, down_rank_projection, preferred_element_type=jnp.float32).astype(jnp.bfloat16)
    live = (jnp.arange(span, dtype=jnp.int32)[None, :] < lengths[:, None]).reshape(examples * span, 1)
    out_live = jnp.where(live, out_side, jnp.zeros_like(out_side))
    rank_a_live = jnp.where(live, rank_a, jnp.zeros_like(rank_a))
    side = out_side.shape[1]
    grad_b = jnp.einsum('nti,ntj->nij', out_live.astype(jnp.float32).reshape(examples, span, side), rank_b.astype(jnp.float32).reshape(examples, span, side), precision=lax.Precision.HIGHEST)
    grad_a = jnp.einsum('nti,ntj->nij', rank_a_live.astype(jnp.float32).reshape(examples, span, side), in_side.astype(jnp.float32).reshape(examples, span, side), precision=lax.Precision.HIGHEST)
    inv_root = lax.rsqrt(jnp.maximum(lengths, 1).astype(jnp.float32))
    stacked = jnp.concatenate([grad_b.reshape(examples, side * side), grad_a.reshape(examples, side * side)], axis=1)
    return stacked * inv_root[:, None]

def reference(activations, cotangent, lengths, handover, adapter_down_factor, adapter_up_factor, output_feature_projection, up_rank_projection, input_feature_projection, down_rank_projection):
    example_features = per_token_features(activations, cotangent, lengths, adapter_down_factor, adapter_up_factor, output_feature_projection, up_rank_projection, input_feature_projection, down_rank_projection)
    kept_share = (1 - handover).astype(jnp.float32)
    own_rows = (example_features * kept_share[:, None]).reshape(N_DP, E_DEV, FEATURES)
    group_plan = handover.reshape(N_DP, E_DEV)
    earlier = jnp.cumsum(group_plan, axis=1) - group_plan
    slot_ids = jnp.arange(MOVED, dtype=jnp.int32)
    chooser = ((group_plan[:, None, :] == 1) & (earlier[:, None, :] == slot_ids[None, :, None])).astype(jnp.float32)
    packed = jnp.einsum('dke,def->dkf', chooser, example_features.reshape(N_DP, E_DEV, FEATURES), precision=lax.Precision.HIGHEST)
    incoming = jnp.roll(packed, 1, axis=0)
    feature_store = jnp.concatenate([own_rows, incoming], axis=1).reshape(STORE, FEATURES)
    gram_panel = jnp.dot(example_features.T, example_features, precision=lax.Precision.HIGHEST, preferred_element_type=jnp.float32)
    gram_panel = gram_panel * (1.0 / math.sqrt(EXAMPLES))
    return (feature_store, gram_panel)
```

```python
import functools
import math

import jax
import jax.numpy as jnp
from jax import lax
from jax.experimental import pallas as pl
from jax.experimental.pallas import tpu as pltpu
from jax.sharding import PartitionSpec as P

MOVED = 2
LANES = 128
DEPTH_CHUNKS = 8
COT_CHUNKS = 2
MESH = pl.DeviceIdType.MESH
F32 = jnp.float32
BF16 = jnp.bfloat16
NT = (((1,), (1,)), ((), ()))
TN = (((0,), (0,)), ((), ()))


def features_kernel(
    n, lengths_ref, handover_ref, act_ref, cot_ref, down_ref, up_ref, outp_ref, upr_ref, inp_ref,
    downr_ref, full_ref, rows_ref, act, cot, w_in, w_out, w_b, w_a, acc, block, inter, packed,
    arrived, act_sem, cot_sem, w_sem, z_send, y_send, core_send, recv, next_send, next_recv,
):
    examples = lengths_ref.shape[0]
    tokens, width = act_ref.shape
    span = tokens // examples
    side = down_ref.shape[0]
    out_width = cot_ref.shape[1]
    me = lax.axis_index("dp")
    group = lax.axis_index("groups")
    lines = n // 4
    z, y, c = me // 4, (me // 2) % 2, me % 2

    def at(zz, yy, cc):
        return zz * 4 + yy * 2 + cc

    def flip(value, mask):
        bit = 1
        while bit <= mask:
            if mask & bit:
                value = value + bit - 2 * bit * ((value // bit) % 2)
            bit *= 2
        return value

    others = [flip(z, d) for d in range(1, lines)]
    core_mate, y_mate = at(z, y, 1 - c), at(z, 1 - y, c)
    after, before = lax.rem(me + 1, n), lax.rem(me + n - 1, n)

    barrier = pltpu.get_barrier_semaphore()
    mates = [core_mate, y_mate, after, before] + [at(o, y, c) for o in others]
    for mate in mates:
        pl.semaphore_signal(barrier, inc=1, device_id=(group, mate), device_id_type=MESH)

    w_copies = [
        pltpu.make_async_copy(outp_ref, w_out.at[:side], w_sem.at[0]),
        pltpu.make_async_copy(up_ref, w_out.at[side:], w_sem.at[1]),
        pltpu.make_async_copy(down_ref, w_in.at[:side], w_sem.at[2]),
        pltpu.make_async_copy(inp_ref, w_in.at[side:], w_sem.at[3]),
    ]
    cot_step = tokens // COT_CHUNKS
    cot_copies = [
        pltpu.make_async_copy(
            cot_ref.at[pl.ds(i * cot_step, cot_step)], cot.at[pl.ds(i * cot_step, cot_step)],
            cot_sem.at[i],
        )
        for i in range(COT_CHUNKS)
    ]
    step = width // DEPTH_CHUNKS
    act_copies = [
        pltpu.make_async_copy(
            act_ref.at[:, pl.ds(i * step, step)], act.at[:, pl.ds(i * step, step)], act_sem.at[i]
        )
        for i in range(DEPTH_CHUNKS)
    ]
    for copy in w_copies[:2] + cot_copies + w_copies[2:] + act_copies:
        copy.start()

    w_b[...] = jnp.zeros_like(w_b)
    w_a[...] = jnp.zeros_like(w_a)
    w_b[:side, :side] = upr_ref[...]
    w_a[side:, side:] = downr_ref[...]

    lane = lax.broadcasted_iota(jnp.int32, (cot_step, LANES), 1)
    w_copies[0].wait()
    w_copies[1].wait()
    left = []
    for i in range(COT_CHUNKS):
        cot_copies[i].wait()
        both = lax.dot_general(
            cot[pl.ds(i * cot_step, cot_step)], w_out[...], NT, preferred_element_type=F32
        ).astype(BF16)
        rank_a = jnp.dot(both, w_a[...], preferred_element_type=F32).astype(BF16)
        left.append(jnp.where(lane < side, both.astype(F32), rank_a.astype(F32)))

    w_copies[2].wait()
    w_copies[3].wait()
    for i in range(DEPTH_CHUNKS):
        act_copies[i].wait()
        cols = pl.ds(i * step, step)
        part = lax.dot_general(act[:, cols], w_in[:, cols], NT, preferred_element_type=F32)
        if i == 0:
            acc[...] = part
        else:
            acc[...] += part

    half_lane = lax.broadcasted_iota(jnp.int32, (side // 2, LANES), 1) < side
    span_lane = lax.broadcasted_iota(jnp.int32, (span, LANES), 1) < side
    span_row = lax.broadcasted_iota(jnp.int32, (span, LANES), 0)
    per_chunk = cot_step // span
    earlier = jnp.int32(0)
    moved = [None] * MOVED
    for e in range(examples):
        rows = pl.ds(e * span, span)
        both = acc[rows].astype(BF16)
        rank_b = jnp.dot(both, w_b[...], preferred_element_type=F32).astype(BF16)
        right = jnp.where(span_lane, rank_b.astype(F32), both.astype(F32)).astype(BF16)
        at_row = (e % per_chunk) * span
        mine = left[e // per_chunk][at_row : at_row + span]
        live = jnp.where(span_row < lengths_ref[e], mine, 0.0).astype(BF16)
        root = lax.rsqrt(jnp.full((1, LANES), jnp.maximum(lengths_ref[e], 1).astype(F32)))
        block[e] = lax.dot_general(live, right, TN, preferred_element_type=F32) * root
        even = block[e, pl.ds(0, side, stride=2), :]
        odd = block[e, pl.ds(1, side, stride=2), :]
        half = side // 2
        top = jnp.where(half_lane, even[:half], pltpu.roll(odd[:half], LANES // 2, 1))
        low = jnp.where(half_lane, pltpu.roll(even[half:], LANES // 2, 1), odd[half:])
        flat = jnp.concatenate([top, low], axis=0)
        inter[pl.ds(e, side, stride=examples), :] = flat
        hand = handover_ref[e]
        rows_ref[pl.ds(e, side, stride=8), :] = flat * (1 - hand).astype(F32)
        for m in range(MOVED):
            share = jnp.where((hand == 1) & (earlier == m), 1.0, 0.0).astype(F32)
            term = flat * share
            moved[m] = term if moved[m] is None else moved[m] + term
        earlier = earlier + hand
    for m in range(MOVED):
        packed[m * side : (m + 1) * side] = moved[m].astype(BF16)
    full_ref[me] = inter[...].astype(BF16).reshape(full_ref.shape[1:])

    pl.semaphore_wait(barrier, len(mates))

    def send(slot, sem, mate):
        return pltpu.make_async_remote_copy(
            src_ref=full_ref.at[slot], dst_ref=full_ref.at[slot], send_sem=sem,
            recv_sem=recv.at[slot], device_id=(group, mate), device_id_type=MESH,
        )

    def landed(slot):
        send(slot, core_send.at[0], core_mate).wait_recv()

    started = []

    def go(slot, sem, mate):
        copy = send(slot, sem, mate)
        copy.start()
        started.append(copy)

    go(me, y_send.at[0], y_mate)
    for d, o in enumerate(others):
        go(me, z_send.at[d], at(o, y, c))
    go(me, core_send.at[0], core_mate)
    hop = pltpu.make_async_remote_copy(
        src_ref=packed, dst_ref=arrived, send_sem=next_send, recv_sem=next_recv,
        device_id=(group, after), device_id_type=MESH,
    )
    hop.start()
    for d, o in enumerate(others):
        slot = at(o, y, c)
        landed(slot)
        go(slot, y_send.at[1 + d], y_mate)
        go(slot, core_send.at[1 + d], core_mate)
    for d, o in enumerate([z] + others):
        slot = at(o, 1 - y, c)
        landed(slot)
        go(slot, core_send.at[lines + d], core_mate)
    hop.wait_recv()
    for m in range(MOVED):
        rows_ref[pl.ds(examples + m, side, stride=8), :] = arrived[
            m * side : (m + 1) * side
        ].astype(F32)
    for row in range(examples + MOVED, 8):
        rows_ref[pl.ds(row, side, stride=8), :] = jnp.zeros((side, LANES), F32)
    for o in [z] + others:
        landed(at(o, y, 1 - c))
    for o in [z] + others:
        landed(at(o, 1 - y, 1 - c))
    hop.wait_send()
    for copy in started:
        copy.wait_send()


def gram_kernel(n, examples, scale, full_ref, rows_ref, store_ref, gram_ref, panel):
    me = lax.axis_index("dp")
    j = pl.program_id(0)
    blocks = gram_ref.shape[0] // LANES
    depth = n * 16
    per_tile = 16 // examples

    @pl.when(j == 0)
    def _():
        lane = lax.broadcasted_iota(jnp.int32, (LANES, LANES), 1)
        for t in range(blocks):
            block = me * blocks + t
            place = t % per_tile if blocks % per_tile == 0 else block % per_tile
            columns = full_ref[:, block // per_tile].reshape(depth, LANES).astype(F32)
            for q in range(depth // LANES):
                turned = columns[q * LANES : (q + 1) * LANES].T * scale
                for m in range(per_tile):
                    shift = (examples * (m - place) + LANES) % LANES
                    moved = turned
                    if not isinstance(shift, int) or shift:
                        moved = pltpu.roll(turned, shift, 1)
                    keep = (lane // examples) % per_tile == m
                    panel[m, t * LANES : (t + 1) * LANES, q * LANES : (q + 1) * LANES] = jnp.where(
                        keep, moved, 0.0
                    ).astype(BF16)
        height = store_ref.shape[0]
        for r in range(store_ref.shape[1] // LANES):
            store_ref[:, r * LANES : (r + 1) * LANES] = rows_ref[r * 8 : r * 8 + height, :]

    tiles = gram_ref.shape[1] // (LANES * per_tile)
    right = jnp.concatenate(
        [full_ref[:, j * tiles + t].reshape(depth, LANES) for t in range(tiles)], axis=1
    )
    for m in range(per_tile):
        product = jnp.dot(panel[m], right, preferred_element_type=F32)
        for t in range(tiles):
            column = (t * per_tile + m) * LANES
            gram_ref[:, column : column + LANES] = product[:, t * LANES : (t + 1) * LANES]


def shards(
    activations,
    cotangent,
    lengths,
    handover,
    adapter_down_factor,
    adapter_up_factor,
    output_feature_projection,
    up_rank_projection,
    input_feature_projection,
    down_rank_projection,
):
    n = lax.axis_size("dp")
    examples, span, width = activations.shape
    out_width = cotangent.shape[2]
    side = input_feature_projection.shape[1]
    tokens = examples * span
    feature_width = 2 * side * side
    tiles = feature_width // LANES * examples // 16
    dma = pltpu.SemaphoreType.DMA
    vmem = pl.BlockSpec(memory_space=pltpu.VMEM)
    smem = pl.BlockSpec(memory_space=pltpu.SMEM)
    far = pl.BlockSpec(memory_space=pl.ANY)
    full, rows = pl.pallas_call(
        functools.partial(features_kernel, n),
        out_shape=(
            jax.ShapeDtypeStruct((n, tiles, 16, LANES), BF16),
            jax.ShapeDtypeStruct((feature_width // LANES * 8, LANES), F32),
        ),
        in_specs=[smem, smem, far, far, far, far, far, vmem, far, vmem],
        out_specs=(vmem, vmem),
        scratch_shapes=[
            pltpu.VMEM((tokens, width), BF16),
            pltpu.VMEM((tokens, out_width), BF16),
            pltpu.VMEM((2 * side, width), BF16),
            pltpu.VMEM((2 * side, out_width), BF16),
            pltpu.VMEM((2 * side, 2 * side), BF16),
            pltpu.VMEM((2 * side, 2 * side), BF16),
            pltpu.VMEM((tokens, LANES), F32),
            pltpu.VMEM((examples, 2 * side, LANES), F32),
            pltpu.VMEM((examples * side, LANES), F32),
            pltpu.VMEM((MOVED * side, LANES), BF16),
            pltpu.VMEM((MOVED * side, LANES), BF16),
            dma((DEPTH_CHUNKS,)),
            dma((COT_CHUNKS,)),
            dma((4,)),
            dma((n // 4,)),
            dma((n // 4,)),
            dma((n // 2,)),
            dma((n,)),
            dma,
            dma,
        ],
        compiler_params=pltpu.CompilerParams(
            collective_id=0, has_side_effects=True, vmem_limit_bytes=48 * 2**20
        ),
        name="features",
    )(
        lengths,
        handover,
        activations.reshape(tokens, width),
        cotangent.reshape(tokens, out_width),
        adapter_down_factor,
        adapter_up_factor.T,
        output_feature_projection.T,
        up_rank_projection,
        input_feature_projection.T,
        down_rank_projection,
    )
    panel_width = feature_width // n
    grid = 8
    scale = 1.0 / math.sqrt(examples * n)
    return pl.pallas_call(
        functools.partial(gram_kernel, n, examples, scale),
        out_shape=(
            jax.ShapeDtypeStruct((examples + MOVED, feature_width), F32),
            jax.ShapeDtypeStruct((panel_width, feature_width), F32),
        ),
        grid=(grid,),
        in_specs=[vmem, vmem],
        out_specs=(
            pl.BlockSpec((examples + MOVED, feature_width), lambda j: (0, 0)),
            pl.BlockSpec((panel_width, feature_width // grid), lambda j: (0, j)),
        ),
        scratch_shapes=[pltpu.VMEM((16 // examples, panel_width, n * 16), BF16)],
        compiler_params=pltpu.CompilerParams(vmem_limit_bytes=32 * 2**20),
        name="gram",
    )(full, rows)


def solution(mesh):
    in_specs = (
        P(("groups", "dp"), None, None),
        P(("groups", "dp"), None, None),
        P(("groups", "dp")),
        P(("groups", "dp")),
        P(),
        P(),
        P(),
        P(),
        P(),
        P(),
    )
    out_specs = (P(("groups", "dp"), None), P(("groups", "dp"), None))
    return jax.shard_map(shards, mesh=mesh, in_specs=in_specs, out_specs=out_specs, check_vma=False)
```

```python
import functools
import math

import jax
import jax.numpy as jnp
from jax import lax
from jax.experimental import pallas as pl
from jax.experimental.pallas import tpu as pltpu
from jax.sharding import PartitionSpec as P

MOVED = 2
LANES = 128
DEPTH_CHUNKS = 8
COT_CHUNKS = 2
MESH = pl.DeviceIdType.MESH
F32 = jnp.float32
BF16 = jnp.bfloat16
NT = (((1,), (1,)), ((), ()))
TN = (((0,), (0,)), ((), ()))


def features_kernel(
    n, lengths_in, handover_in, act_ref, cot_ref, down_ref, up_ref, outp_ref, upr_in, inp_ref,
    downr_in, full_ref, rows_out, mine_ref, rows_ref, lengths_ref, handover_ref, upr_ref, downr_ref, act, cot, w_in,
    w_out, w_b, w_a, acc, block, inter, packed, arrived, out_sem, small_sem, act_sem, cot_sem, w_sem, z_send, y_send, core_send, recv, next_send, next_recv,
):
    examples = lengths_in.shape[0]
    tokens, width = act_ref.shape
    span = tokens // examples
    side = down_ref.shape[0]
    out_width = cot_ref.shape[1]
    me = lax.axis_index("dp")
    group = lax.axis_index("groups")
    lines = n // 4
    z, y, c = me // 4, (me // 2) % 2, me % 2

    def at(zz, yy, cc):
        return zz * 4 + yy * 2 + cc

    def flip(value, mask):
        bit = 1
        while bit <= mask:
            if mask & bit:
                value = value + bit - 2 * bit * ((value // bit) % 2)
            bit *= 2
        return value

    others = [flip(z, d) for d in range(1, lines)]
    core_mate, y_mate = at(z, y, 1 - c), at(z, 1 - y, c)
    after, before = lax.rem(me + 1, n), lax.rem(me + n - 1, n)

    barrier = pltpu.get_barrier_semaphore()
    mates = [core_mate, y_mate, after, before] + [at(o, y, c) for o in others]
    for mate in mates:
        pl.semaphore_signal(barrier, inc=1, device_id=(group, mate), device_id_type=MESH)

    w_copies = [
        pltpu.make_async_copy(outp_ref, w_out.at[:side], w_sem.at[0]),
        pltpu.make_async_copy(up_ref, w_out.at[side:], w_sem.at[1]),
        pltpu.make_async_copy(down_ref, w_in.at[:side], w_sem.at[2]),
        pltpu.make_async_copy(inp_ref, w_in.at[side:], w_sem.at[3]),
    ]
    cot_step = tokens // COT_CHUNKS
    cot_copies = [
        pltpu.make_async_copy(
            cot_ref.at[pl.ds(i * cot_step, cot_step)], cot.at[pl.ds(i * cot_step, cot_step)],
            cot_sem.at[i],
        )
        for i in range(COT_CHUNKS)
    ]
    step = width // DEPTH_CHUNKS
    act_copies = [
        pltpu.make_async_copy(
            act_ref.at[:, pl.ds(i * step, step)], act.at[:, pl.ds(i * step, step)], act_sem.at[i]
        )
        for i in range(DEPTH_CHUNKS)
    ]
    small = [
        pltpu.make_async_copy(source, target, small_sem.at[i])
        for i, (source, target) in enumerate(
            [
                (upr_in, upr_ref),
                (downr_in, downr_ref),
                (lengths_in, lengths_ref),
                (handover_in, handover_ref),
            ]
        )
    ]
    for copy in w_copies[:2] + small + cot_copies + w_copies[2:] + act_copies:
        copy.start()

    w_b[...] = jnp.zeros_like(w_b)
    w_a[...] = jnp.zeros_like(w_a)
    for copy in small:
        copy.wait()
    w_b[:side, :side] = upr_ref[...]
    w_a[side:, side:] = downr_ref[...]

    lane = lax.broadcasted_iota(jnp.int32, (cot_step, LANES), 1)
    w_copies[0].wait()
    w_copies[1].wait()
    left = []
    for i in range(COT_CHUNKS):
        cot_copies[i].wait()
        both = lax.dot_general(
            cot[pl.ds(i * cot_step, cot_step)], w_out[...], NT, preferred_element_type=F32
        ).astype(BF16)
        rank_a = jnp.dot(both, w_a[...], preferred_element_type=F32).astype(BF16)
        left.append(jnp.where(lane < side, both.astype(F32), rank_a.astype(F32)))

    w_copies[2].wait()
    w_copies[3].wait()
    for i in range(DEPTH_CHUNKS):
        act_copies[i].wait()
        cols = pl.ds(i * step, step)
        part = lax.dot_general(act[:, cols], w_in[:, cols], NT, preferred_element_type=F32)
        if i == 0:
            acc[...] = part
        else:
            acc[...] += part

    half_lane = lax.broadcasted_iota(jnp.int32, (side // 2, LANES), 1) < side
    span_lane = lax.broadcasted_iota(jnp.int32, (span, LANES), 1) < side
    span_row = lax.broadcasted_iota(jnp.int32, (span, LANES), 0)
    per_chunk = cot_step // span
    earlier = jnp.int32(0)
    moved = [None] * MOVED
    for e in range(examples):
        rows = pl.ds(e * span, span)
        both = acc[rows].astype(BF16)
        rank_b = jnp.dot(both, w_b[...], preferred_element_type=F32).astype(BF16)
        right = jnp.where(span_lane, rank_b.astype(F32), both.astype(F32)).astype(BF16)
        at_row = (e % per_chunk) * span
        mine = left[e // per_chunk][at_row : at_row + span]
        live = jnp.where(span_row < lengths_ref[e], mine, 0.0).astype(BF16)
        root = lax.rsqrt(jnp.full((1, LANES), jnp.maximum(lengths_ref[e], 1).astype(F32)))
        block[e] = lax.dot_general(live, right, TN, preferred_element_type=F32) * root
        even = block[e, pl.ds(0, side, stride=2), :]
        odd = block[e, pl.ds(1, side, stride=2), :]
        half = side // 2
        top = jnp.where(half_lane, even[:half], pltpu.roll(odd[:half], LANES // 2, 1))
        low = jnp.where(half_lane, pltpu.roll(even[half:], LANES // 2, 1), odd[half:])
        flat = jnp.concatenate([top, low], axis=0)
        inter[pl.ds(e, side, stride=examples), :] = flat
        hand = handover_ref[e]
        rows_ref[pl.ds(e, side, stride=8), :] = flat * (1 - hand).astype(F32)
        for m in range(MOVED):
            share = jnp.where((hand == 1) & (earlier == m), 1.0, 0.0).astype(F32)
            term = flat * share
            moved[m] = term if moved[m] is None else moved[m] + term
        earlier = earlier + hand
    for m in range(MOVED):
        packed[m * side : (m + 1) * side] = moved[m].astype(BF16)
    mine_ref[...] = inter[...].astype(BF16).reshape(mine_ref.shape)
    keep = pltpu.make_async_copy(mine_ref, full_ref.at[me], out_sem.at[0])
    keep.start()

    pl.semaphore_wait(barrier, len(mates))

    def send(slot, sem, mate, own=False):
        return pltpu.make_async_remote_copy(
            src_ref=mine_ref if own else full_ref.at[slot], dst_ref=full_ref.at[slot], send_sem=sem,
            recv_sem=recv.at[slot], device_id=(group, mate), device_id_type=MESH,
        )

    def landed(slot):
        send(slot, core_send.at[0], core_mate).wait_recv()

    started = []

    def go(slot, sem, mate, own=False):
        copy = send(slot, sem, mate, own)
        copy.start()
        started.append(copy)

    go(me, y_send.at[0], y_mate, True)
    for d, o in enumerate(others):
        go(me, z_send.at[d], at(o, y, c), True)
    go(me, core_send.at[0], core_mate, True)
    hop = pltpu.make_async_remote_copy(
        src_ref=packed, dst_ref=arrived, send_sem=next_send, recv_sem=next_recv,
        device_id=(group, after), device_id_type=MESH,
    )
    hop.start()
    for d, o in enumerate(others):
        slot = at(o, y, c)
        landed(slot)
        go(slot, y_send.at[1 + d], y_mate)
        go(slot, core_send.at[1 + d], core_mate)
    for d, o in enumerate([z] + others):
        slot = at(o, 1 - y, c)
        landed(slot)
        go(slot, core_send.at[lines + d], core_mate)
    hop.wait_recv()
    for m in range(MOVED):
        rows_ref[pl.ds(examples + m, side, stride=8), :] = arrived[
            m * side : (m + 1) * side
        ].astype(F32)
    for row in range(examples + MOVED, 8):
        rows_ref[pl.ds(row, side, stride=8), :] = jnp.zeros((side, LANES), F32)
    keep_rows = pltpu.make_async_copy(rows_ref, rows_out, out_sem.at[1])
    keep_rows.start()
    for o in [z] + others:
        landed(at(o, y, 1 - c))
    for o in [z] + others:
        landed(at(o, 1 - y, 1 - c))
    hop.wait_send()
    keep.wait()
    keep_rows.wait()
    for copy in started:
        copy.wait_send()


def gram_kernel(
    n, examples, scale, full_in, rows_in, store_ref, gram_ref, panel, full_ref, rows_ref, sem
):
    me = lax.axis_index("dp")
    j = pl.program_id(0)
    blocks = gram_ref.shape[0] // LANES
    depth = n * 16
    per_tile = 16 // examples

    @pl.when(j == 0)
    def _():
        fetch = pltpu.make_async_copy(full_in, full_ref, sem.at[0])
        fetch.start()
        pltpu.make_async_copy(rows_in, rows_ref, sem.at[1]).start()
        fetch.wait()
        lane = lax.broadcasted_iota(jnp.int32, (LANES, LANES), 1)
        for t in range(blocks):
            block = me * blocks + t
            place = t % per_tile if blocks % per_tile == 0 else block % per_tile
            columns = full_ref[:, block // per_tile].reshape(depth, LANES).astype(F32)
            for q in range(depth // LANES):
                turned = columns[q * LANES : (q + 1) * LANES].T * scale
                for m in range(per_tile):
                    shift = (examples * (m - place) + LANES) % LANES
                    moved = turned
                    if not isinstance(shift, int) or shift:
                        moved = pltpu.roll(turned, shift, 1)
                    keep = (lane // examples) % per_tile == m
                    panel[m, t * LANES : (t + 1) * LANES, q * LANES : (q + 1) * LANES] = jnp.where(
                        keep, moved, 0.0
                    ).astype(BF16)

    @pl.when(j == 1)
    def _():
        pltpu.make_async_copy(rows_in, rows_ref, sem.at[1]).wait()
        height = store_ref.shape[0]
        for r in range(store_ref.shape[1] // LANES):
            store_ref[:, r * LANES : (r + 1) * LANES] = rows_ref[r * 8 : r * 8 + height, :]

    tiles = gram_ref.shape[1] // (LANES * per_tile)
    right = jnp.concatenate(
        [full_ref[:, j * tiles + t].reshape(depth, LANES) for t in range(tiles)], axis=1
    )
    for m in range(per_tile):
        product = jnp.dot(panel[m], right, preferred_element_type=F32)
        for t in range(tiles):
            column = (t * per_tile + m) * LANES
            gram_ref[:, column : column + LANES] = product[:, t * LANES : (t + 1) * LANES]


def shards(
    activations,
    cotangent,
    lengths,
    handover,
    adapter_down_factor,
    adapter_up_factor,
    output_feature_projection,
    up_rank_projection,
    input_feature_projection,
    down_rank_projection,
):
    n = lax.axis_size("dp")
    examples, span, width = activations.shape
    out_width = cotangent.shape[2]
    side = input_feature_projection.shape[1]
    tokens = examples * span
    feature_width = 2 * side * side
    tiles = feature_width // LANES * examples // 16
    dma = pltpu.SemaphoreType.DMA
    far = pl.BlockSpec(memory_space=pl.ANY)
    full, rows = pl.pallas_call(
        functools.partial(features_kernel, n),
        out_shape=(
            jax.ShapeDtypeStruct((n, tiles, 16, LANES), BF16),
            jax.ShapeDtypeStruct((feature_width // LANES * 8, LANES), F32),
        ),
        in_specs=[far] * 10,
        out_specs=(far, far),
        scratch_shapes=[
            pltpu.VMEM((tiles, 16, LANES), BF16),
            pltpu.VMEM((feature_width // LANES * 8, LANES), F32),
            pltpu.SMEM((examples,), jnp.int32),
            pltpu.SMEM((examples,), jnp.int32),
            pltpu.VMEM((side, side), BF16),
            pltpu.VMEM((side, side), BF16),
            pltpu.VMEM((tokens, width), BF16),
            pltpu.VMEM((tokens, out_width), BF16),
            pltpu.VMEM((2 * side, width), BF16),
            pltpu.VMEM((2 * side, out_width), BF16),
            pltpu.VMEM((2 * side, 2 * side), BF16),
            pltpu.VMEM((2 * side, 2 * side), BF16),
            pltpu.VMEM((tokens, LANES), F32),
            pltpu.VMEM((examples, 2 * side, LANES), F32),
            pltpu.VMEM((examples * side, LANES), F32),
            pltpu.VMEM((MOVED * side, LANES), BF16),
            pltpu.VMEM((MOVED * side, LANES), BF16),
            dma((2,)),
            dma((4,)),
            dma((DEPTH_CHUNKS,)),
            dma((COT_CHUNKS,)),
            dma((4,)),
            dma((n // 4,)),
            dma((n // 4,)),
            dma((n // 2,)),
            dma((n,)),
            dma,
            dma,
        ],
        compiler_params=pltpu.CompilerParams(
            collective_id=0, has_side_effects=True, vmem_limit_bytes=60 * 2**20
        ),
        name="features",
    )(
        lengths,
        handover,
        activations.reshape(tokens, width),
        cotangent.reshape(tokens, out_width),
        adapter_down_factor,
        adapter_up_factor.T,
        output_feature_projection.T,
        up_rank_projection,
        input_feature_projection.T,
        down_rank_projection,
    )
    panel_width = feature_width // n
    grid = 8
    scale = 1.0 / math.sqrt(examples * n)
    return pl.pallas_call(
        functools.partial(gram_kernel, n, examples, scale),
        out_shape=(
            jax.ShapeDtypeStruct((examples + MOVED, feature_width), F32),
            jax.ShapeDtypeStruct((panel_width, feature_width), F32),
        ),
        grid=(grid,),
        in_specs=[far, far],
        out_specs=(
            pl.BlockSpec((examples + MOVED, feature_width), lambda j: (0, 0)),
            pl.BlockSpec((panel_width, feature_width // grid), lambda j: (0, j)),
        ),
        scratch_shapes=[
            pltpu.VMEM((16 // examples, panel_width, n * 16), BF16),
            pltpu.VMEM(full.shape, BF16),
            pltpu.VMEM(rows.shape, F32),
            dma((2,)),
        ],
        compiler_params=pltpu.CompilerParams(vmem_limit_bytes=60 * 2**20),
        name="gram",
    )(full, rows)


def solution(mesh):
    in_specs = (
        P(("groups", "dp"), None, None),
        P(("groups", "dp"), None, None),
        P(("groups", "dp")),
        P(("groups", "dp")),
        P(),
        P(),
        P(),
        P(),
        P(),
        P(),
    )
    out_specs = (P(("groups", "dp"), None), P(("groups", "dp"), None))
    return jax.shard_map(shards, mesh=mesh, in_specs=in_specs, out_specs=out_specs, check_vma=False)
```

```python
import functools
import math

import jax
import jax.numpy as jnp
from jax import lax
from jax.experimental import pallas as pl
from jax.experimental.pallas import tpu as pltpu
from jax.sharding import PartitionSpec as P

MOVED = 2
LANES = 128
DEPTH_CHUNKS = 4
COT_CHUNKS = 2
MESH = pl.DeviceIdType.MESH
F32 = jnp.float32
BF16 = jnp.bfloat16
NT = (((1,), (1,)), ((), ()))
TN = (((0,), (0,)), ((), ()))


def features_kernel(
    n, lengths_in, handover_in, act_ref, cot_ref, down_ref, up_ref, outp_ref, upr_in, inp_ref,
    downr_in, full_ref, rows_out, mine_ref, rows_ref, lengths_ref, handover_ref, upr_ref, downr_ref, act, cot, w_in,
    w_out, w_b, w_a, acc, block, inter, packed, arrived, out_sem, small_sem, act_sem, cot_sem, w_sem, z_send, y_send, core_send, recv, next_send, next_recv,
):
    examples = lengths_in.shape[0]
    tokens, width = act_ref.shape
    span = tokens // examples
    side = down_ref.shape[0]
    out_width = cot_ref.shape[1]
    me = lax.axis_index("dp")
    group = lax.axis_index("groups")
    lines = n // 4
    z, y, c = me // 4, (me // 2) % 2, me % 2

    def at(zz, yy, cc):
        return zz * 4 + yy * 2 + cc

    def flip(value, mask):
        bit = 1
        while bit <= mask:
            if mask & bit:
                value = value + bit - 2 * bit * ((value // bit) % 2)
            bit *= 2
        return value

    others = [flip(z, d) for d in range(1, lines)]
    core_mate, y_mate = at(z, y, 1 - c), at(z, 1 - y, c)
    after, before = lax.rem(me + 1, n), lax.rem(me + n - 1, n)

    barrier = pltpu.get_barrier_semaphore()
    mates = [core_mate, y_mate, after, before] + [at(o, y, c) for o in others]
    for mate in mates:
        pl.semaphore_signal(barrier, inc=1, device_id=(group, mate), device_id_type=MESH)

    w_copies = [
        pltpu.make_async_copy(outp_ref, w_out.at[:side], w_sem.at[0]),
        pltpu.make_async_copy(up_ref, w_out.at[side:], w_sem.at[1]),
        pltpu.make_async_copy(down_ref, w_in.at[:side], w_sem.at[2]),
        pltpu.make_async_copy(inp_ref, w_in.at[side:], w_sem.at[3]),
    ]
    cot_step = tokens // COT_CHUNKS
    cot_copies = [
        pltpu.make_async_copy(
            cot_ref.at[pl.ds(i * cot_step, cot_step)], cot.at[pl.ds(i * cot_step, cot_step)],
            cot_sem.at[i],
        )
        for i in range(COT_CHUNKS)
    ]
    step = width // DEPTH_CHUNKS
    act_copies = [
        pltpu.make_async_copy(
            act_ref.at[:, pl.ds(i * step, step)], act.at[:, pl.ds(i * step, step)], act_sem.at[i]
        )
        for i in range(DEPTH_CHUNKS)
    ]
    small = [
        pltpu.make_async_copy(source, target, small_sem.at[i])
        for i, (source, target) in enumerate(
            [
                (upr_in, upr_ref),
                (downr_in, downr_ref),
                (lengths_in, lengths_ref),
                (handover_in, handover_ref),
            ]
        )
    ]
    for copy in w_copies[:2] + small + cot_copies + w_copies[2:] + act_copies:
        copy.start()

    w_b[...] = jnp.zeros_like(w_b)
    w_a[...] = jnp.zeros_like(w_a)
    for copy in small:
        copy.wait()
    w_b[:side, :side] = upr_ref[...]
    w_a[side:, side:] = downr_ref[...]

    lane = lax.broadcasted_iota(jnp.int32, (cot_step, LANES), 1)
    w_copies[0].wait()
    w_copies[1].wait()
    left = []
    for i in range(COT_CHUNKS):
        cot_copies[i].wait()
        both = lax.dot_general(
            cot[pl.ds(i * cot_step, cot_step)], w_out[...], NT, preferred_element_type=F32
        ).astype(BF16)
        rank_a = jnp.dot(both, w_a[...], preferred_element_type=F32).astype(BF16)
        left.append(jnp.where(lane < side, both.astype(F32), rank_a.astype(F32)))

    span_row = lax.broadcasted_iota(jnp.int32, (span, LANES), 0)
    per_chunk = cot_step // span
    lives = []
    for e in range(examples):
        at_row = (e % per_chunk) * span
        mine = left[e // per_chunk][at_row : at_row + span]
        lives.append(jnp.where(span_row < lengths_ref[e], mine, 0.0).astype(BF16))

    w_copies[2].wait()
    w_copies[3].wait()
    for i in range(DEPTH_CHUNKS):
        act_copies[i].wait()
        cols = pl.ds(i * step, step)
        part = lax.dot_general(act[:, cols], w_in[:, cols], NT, preferred_element_type=F32)
        if i == 0:
            acc[...] = part
        else:
            acc[...] += part

    half_lane = lax.broadcasted_iota(jnp.int32, (side // 2, LANES), 1) < side
    earlier = jnp.int32(0)
    moved = [None] * MOVED
    whole = acc[...].astype(BF16)
    rank_b = jnp.dot(whole, w_b[...], preferred_element_type=F32).astype(BF16)
    all_lane = lax.broadcasted_iota(jnp.int32, (tokens, LANES), 1) < side
    right = jnp.where(all_lane, rank_b.astype(F32), whole.astype(F32)).astype(BF16)
    for e in range(examples):
        root = lax.rsqrt(jnp.full((1, LANES), jnp.maximum(lengths_ref[e], 1).astype(F32)))
        block[e] = (
            lax.dot_general(
                lives[e], right[e * span : (e + 1) * span], TN, preferred_element_type=F32
            )
            * root
        )
    for e in range(examples):
        even = block[e, pl.ds(0, side, stride=2), :]
        odd = block[e, pl.ds(1, side, stride=2), :]
        half = side // 2
        top = jnp.where(half_lane, even[:half], pltpu.roll(odd[:half], LANES // 2, 1))
        low = jnp.where(half_lane, pltpu.roll(even[half:], LANES // 2, 1), odd[half:])
        flat = jnp.concatenate([top, low], axis=0)
        inter[pl.ds(e, side, stride=examples), :] = flat
        hand = handover_ref[e]
        rows_ref[pl.ds(e, side, stride=8), :] = flat * (1 - hand).astype(F32)
        for m in range(MOVED):
            share = jnp.where((hand == 1) & (earlier == m), 1.0, 0.0).astype(F32)
            term = flat * share
            moved[m] = term if moved[m] is None else moved[m] + term
        earlier = earlier + hand
    for m in range(MOVED):
        packed[m * side : (m + 1) * side] = moved[m].astype(BF16)
    mine_ref[...] = inter[...].astype(BF16).reshape(mine_ref.shape)
    keep = pltpu.make_async_copy(mine_ref, full_ref.at[me], out_sem.at[0])
    keep.start()

    pl.semaphore_wait(barrier, len(mates))

    def send(slot, sem, mate, own=False):
        return pltpu.make_async_remote_copy(
            src_ref=mine_ref if own else full_ref.at[slot], dst_ref=full_ref.at[slot], send_sem=sem,
            recv_sem=recv.at[slot], device_id=(group, mate), device_id_type=MESH,
        )

    def landed(slot):
        send(slot, core_send.at[0], core_mate).wait_recv()

    started = []

    def go(slot, sem, mate, own=False):
        copy = send(slot, sem, mate, own)
        copy.start()
        started.append(copy)

    go(me, y_send.at[0], y_mate, True)
    for d, o in enumerate(others):
        go(me, z_send.at[d], at(o, y, c), True)
    go(me, core_send.at[0], core_mate, True)
    hop = pltpu.make_async_remote_copy(
        src_ref=packed, dst_ref=arrived, send_sem=next_send, recv_sem=next_recv,
        device_id=(group, after), device_id_type=MESH,
    )
    hop.start()
    for d, o in enumerate(others):
        slot = at(o, y, c)
        landed(slot)
        go(slot, y_send.at[1 + d], y_mate)
        go(slot, core_send.at[1 + d], core_mate)
    for d, o in enumerate([z] + others):
        slot = at(o, 1 - y, c)
        landed(slot)
        go(slot, core_send.at[lines + d], core_mate)
    hop.wait_recv()
    for m in range(MOVED):
        rows_ref[pl.ds(examples + m, side, stride=8), :] = arrived[
            m * side : (m + 1) * side
        ].astype(F32)
    for row in range(examples + MOVED, 8):
        rows_ref[pl.ds(row, side, stride=8), :] = jnp.zeros((side, LANES), F32)
    keep_rows = pltpu.make_async_copy(rows_ref, rows_out, out_sem.at[1])
    keep_rows.start()
    for o in [z] + others:
        landed(at(o, y, 1 - c))
    for o in [z] + others:
        landed(at(o, 1 - y, 1 - c))
    hop.wait_send()
    keep.wait()
    keep_rows.wait()
    for copy in started:
        copy.wait_send()


def gram_kernel(
    n, examples, scale, full_in, rows_in, store_ref, gram_ref, panel, full_ref, own_ref, rows_ref, sem
):
    me = lax.axis_index("dp")
    j = pl.program_id(0)
    blocks = gram_ref.shape[0] // LANES
    depth = n * 16
    per_tile = 16 // examples
    tiles = gram_ref.shape[1] // (LANES * per_tile)
    own = me * blocks // per_tile
    parts = full_in.shape[1] // tiles

    def part(i):
        cols = pl.ds(i * tiles, tiles)
        return pltpu.make_async_copy(full_in.at[:, cols], full_ref.at[:, cols], sem.at[2 + i])

    @pl.when(j == 0)
    def _():
        source = full_in.at[:, pl.ds(own, 1)]
        first = pltpu.make_async_copy(source, own_ref, sem.at[0])
        first.start()
        for i in range(parts):
            part(i).start()
        pltpu.make_async_copy(rows_in, rows_ref, sem.at[1]).start()
        first.wait()
        lane = lax.broadcasted_iota(jnp.int32, (LANES, LANES), 1)
        for t in range(blocks):
            block = me * blocks + t
            place = t % per_tile if blocks % per_tile == 0 else block % per_tile
            columns = own_ref[:, t // per_tile].reshape(depth, LANES).astype(F32)
            for q in range(depth // LANES):
                turned = columns[q * LANES : (q + 1) * LANES].T * scale
                for m in range(per_tile):
                    shift = (examples * (m - place) + LANES) % LANES
                    moved = turned
                    if not isinstance(shift, int) or shift:
                        moved = pltpu.roll(turned, shift, 1)
                    keep = (lane // examples) % per_tile == m
                    panel[m, t * LANES : (t + 1) * LANES, q * LANES : (q + 1) * LANES] = jnp.where(
                        keep, moved, 0.0
                    ).astype(BF16)

    @pl.when(j == 1)
    def _():
        pltpu.make_async_copy(rows_in, rows_ref, sem.at[1]).wait()
        height = store_ref.shape[0]
        for r in range(store_ref.shape[1] // LANES):
            store_ref[:, r * LANES : (r + 1) * LANES] = rows_ref[r * 8 : r * 8 + height, :]

    part(j).wait()
    right = jnp.concatenate(
        [full_ref[:, j * tiles + t].reshape(depth, LANES) for t in range(tiles)], axis=1
    )
    for m in range(per_tile):
        product = jnp.dot(panel[m], right, preferred_element_type=F32)
        for t in range(tiles):
            column = (t * per_tile + m) * LANES
            gram_ref[:, column : column + LANES] = product[:, t * LANES : (t + 1) * LANES]


def shards(
    activations,
    cotangent,
    lengths,
    handover,
    adapter_down_factor,
    adapter_up_factor,
    output_feature_projection,
    up_rank_projection,
    input_feature_projection,
    down_rank_projection,
):
    n = lax.axis_size("dp")
    examples, span, width = activations.shape
    out_width = cotangent.shape[2]
    side = input_feature_projection.shape[1]
    tokens = examples * span
    feature_width = 2 * side * side
    tiles = feature_width // LANES * examples // 16
    dma = pltpu.SemaphoreType.DMA
    far = pl.BlockSpec(memory_space=pl.ANY)
    full, rows = pl.pallas_call(
        functools.partial(features_kernel, n),
        out_shape=(
            jax.ShapeDtypeStruct((n, tiles, 16, LANES), BF16),
            jax.ShapeDtypeStruct((feature_width // LANES * 8, LANES), F32),
        ),
        in_specs=[far] * 10,
        out_specs=(far, far),
        scratch_shapes=[
            pltpu.VMEM((tiles, 16, LANES), BF16),
            pltpu.VMEM((feature_width // LANES * 8, LANES), F32),
            pltpu.SMEM((examples,), jnp.int32),
            pltpu.SMEM((examples,), jnp.int32),
            pltpu.VMEM((side, side), BF16),
            pltpu.VMEM((side, side), BF16),
            pltpu.VMEM((tokens, width), BF16),
            pltpu.VMEM((tokens, out_width), BF16),
            pltpu.VMEM((2 * side, width), BF16),
            pltpu.VMEM((2 * side, out_width), BF16),
            pltpu.VMEM((2 * side, 2 * side), BF16),
            pltpu.VMEM((2 * side, 2 * side), BF16),
            pltpu.VMEM((tokens, LANES), F32),
            pltpu.VMEM((examples, 2 * side, LANES), F32),
            pltpu.VMEM((examples * side, LANES), F32),
            pltpu.VMEM((MOVED * side, LANES), BF16),
            pltpu.VMEM((MOVED * side, LANES), BF16),
            dma((2,)),
            dma((4,)),
            dma((DEPTH_CHUNKS,)),
            dma((COT_CHUNKS,)),
            dma((4,)),
            dma((n // 4,)),
            dma((n // 4,)),
            dma((n // 2,)),
            dma((n,)),
            dma,
            dma,
        ],
        compiler_params=pltpu.CompilerParams(
            collective_id=0, has_side_effects=True, vmem_limit_bytes=60 * 2**20
        ),
        name="features",
    )(
        lengths,
        handover,
        activations.reshape(tokens, width),
        cotangent.reshape(tokens, out_width),
        adapter_down_factor,
        adapter_up_factor.T,
        output_feature_projection.T,
        up_rank_projection,
        input_feature_projection.T,
        down_rank_projection,
    )
    panel_width = feature_width // n
    grid = 8
    scale = 1.0 / math.sqrt(examples * n)
    return pl.pallas_call(
        functools.partial(gram_kernel, n, examples, scale),
        out_shape=(
            jax.ShapeDtypeStruct((examples + MOVED, feature_width), F32),
            jax.ShapeDtypeStruct((panel_width, feature_width), F32),
        ),
        grid=(grid,),
        in_specs=[far, far],
        out_specs=(
            pl.BlockSpec((examples + MOVED, feature_width), lambda j: (0, 0)),
            pl.BlockSpec((panel_width, feature_width // grid), lambda j: (0, j)),
        ),
        scratch_shapes=[
            pltpu.VMEM((16 // examples, panel_width, n * 16), BF16),
            pltpu.VMEM(full.shape, BF16),
            pltpu.VMEM((n, 1, 16, LANES), BF16),
            pltpu.VMEM(rows.shape, F32),
            dma((2 + grid,)),
        ],
        compiler_params=pltpu.CompilerParams(vmem_limit_bytes=60 * 2**20),
        name="gram",
    )(full, rows)


def solution(mesh):
    in_specs = (
        P(("groups", "dp"), None, None),
        P(("groups", "dp"), None, None),
        P(("groups", "dp")),
        P(("groups", "dp")),
        P(),
        P(),
        P(),
        P(),
        P(),
        P(),
    )
    out_specs = (P(("groups", "dp"), None), P(("groups", "dp"), None))
    return jax.shard_map(shards, mesh=mesh, in_specs=in_specs, out_specs=out_specs, check_vma=False)
```
